32 devices in a mesh: dp: 8 (over z, x), seq: 4 (over y, core).
Axes of the slice: x: 2, y: 2, z: 4, core: 2. Of those that a mesh axis runs over, the one named last changes fastest.
Arguments:
- codes: int32 [8, 8192], P('dp', 'seq'), may hold values from 0 to 3
- embed: bfloat16 [4, 256], replicated, may hold values from -6 to 6
- first_weight_taps: bfloat16 [3, 256, 256], replicated, may hold values from -0.21875 to 0.21875
- second_weight_taps: bfloat16 [3, 256, 256], replicated, may hold values from -0.21875 to 0.21875
- cotangent: bfloat16 [8, 8192, 256], P('dp', 'seq'), may hold values from -6 to 6
Outputs:
- block_out: bfloat16 [8, 8192, 256], P('dp', 'seq')
- first_weight_gradient: float32 [3, 256, 256], replicated
- second_weight_gradient: float32 [3, 256, 256], replicated
The draws below stay inside these ranges and needn't reach their ends.
All inputs are finite; a program needn't handle non-finite values.
Results may differ from the reference program's by a relative error of at most 0.0085.
Values may be sent and summed in bfloat16 or wider, within the bound.
A program may use at most 64 MiB of HBM per device.

```python
import math
import jax
import jax.numpy as jnp
from jax import lax

CHANNELS = 256
FIRST_DILATION = 4
SECOND_DILATION = 16
SEQLEN = 8192
WINDOWS = 8


def draw_cotangent(key, part):
    edge_rows = 32
    inner_scale = math.sqrt(2.0 * edge_rows / (SEQLEN - 2 * edge_rows))
    position = jnp.arange(SEQLEN, dtype=jnp.int32)
    at_edge = (position < edge_rows) | (position >= SEQLEN - edge_rows)
    envelope = jnp.where(at_edge, jnp.float32(1.0), jnp.float32(inner_scale)).astype(jnp.float32)
    extent = (WINDOWS, SEQLEN, CHANNELS)
    values = jnp.clip(jax.random.normal(key, extent, jnp.float32), -6.0, 6.0)
    return (values * envelope[None, :, None]).astype(jnp.bfloat16)


def with_ends(result, own_key, smallest, largest):
    place = [jax.random.randint(jax.random.fold_in(own_key, axis), (), 0, length) for axis, length in enumerate(result.shape)]
    main_axis = result.shape.index(max(result.shape))
    next_to = place[:main_axis] + [(place[main_axis] + 1) % result.shape[main_axis]] + place[main_axis + 1:]
    return result.at[tuple(place)].set(smallest).at[tuple(next_to)].set(largest)


def noise(rng, shape, deviation, reach, kind=jnp.bfloat16):
    entries = jax.random.normal(rng, shape, jnp.float32) * deviation
    return jnp.minimum(jnp.maximum(entries, -reach), reach).astype(kind)


def setup_inputs(seed: int = 0) -> dict:
    keys = jax.random.split(jax.random.key(seed), 6)
    return {
        "codes": with_ends(jax.random.randint(keys[0], (WINDOWS, SEQLEN), 0, 4), jax.random.fold_in(keys[0], 1), 0, 3).astype(jnp.int32),
        "embed": noise(keys[1], (4, CHANNELS), 1.0, 6.0),
        "first_weight_taps": noise(keys[2], (3, CHANNELS, CHANNELS), (3 * CHANNELS) ** -0.5, 0.21875),
        "second_weight_taps": noise(keys[3], (3, CHANNELS, CHANNELS), (3 * CHANNELS) ** -0.5, 0.21875),
        "cotangent": draw_cotangent(jax.random.fold_in(keys[5], 71), 0),
    }


def strand_flip(value):
    return value[::-1, ::-1]

def stack_shifts(value, dilation, order):
    count_rows = value.shape[0]
    padded = jnp.pad(value, ((dilation, dilation), (0, 0)))
    return jnp.concatenate([padded[k * dilation:k * dilation + count_rows] for k in order], axis=-1)

def dilated_filter(value, weight, dilation):
    flat = weight.reshape(-1, weight.shape[2])
    return jnp.dot(stack_shifts(value, dilation, (0, 1, 2)), flat, preferred_element_type=jnp.float32)

def transposed_filter(grad, weight, dilation):
    flat = jnp.transpose(weight, (0, 2, 1)).reshape(-1, weight.shape[2])
    return jnp.dot(stack_shifts(grad, dilation, (2, 1, 0)), flat, preferred_element_type=jnp.float32)

def weight_gradient_total(value, grad, dilation):
    stacked = stack_shifts(value, dilation, (0, 1, 2))
    term = jnp.dot(stacked.T, grad, preferred_element_type=jnp.float32)
    return term.reshape(3, value.shape[1], value.shape[1])

def one_window(codes_row, cot_row, embed, first_weight_taps, second_weight_taps):
    onehot = (codes_row[:, None] == jnp.arange(4, dtype=jnp.int32)[None, :]).astype(jnp.bfloat16)
    nucleotide_features = jnp.dot(onehot, embed, preferred_element_type=jnp.float32).astype(jnp.bfloat16)
    first_activation = dilated_filter(nucleotide_features, first_weight_taps, FIRST_DILATION) + strand_flip(dilated_filter(strand_flip(nucleotide_features), first_weight_taps, FIRST_DILATION))
    gelu_one, back_one = jax.vjp(jax.nn.gelu, first_activation)
    hidden_state = gelu_one.astype(jnp.bfloat16)
    second_activation = dilated_filter(hidden_state, second_weight_taps, SECOND_DILATION) + strand_flip(dilated_filter(strand_flip(hidden_state), second_weight_taps, SECOND_DILATION))
    gelu_two, back_two = jax.vjp(jax.nn.gelu, second_activation)
    block_out = (hidden_state.astype(jnp.float32) + gelu_two).astype(jnp.bfloat16)
    cotangent_wide_float = cot_row.astype(jnp.float32)
    second_activation_gradient = back_two(cotangent_wide_float)[0].astype(jnp.bfloat16)
    hidden_gradient = cotangent_wide_float + transposed_filter(second_activation_gradient, second_weight_taps, SECOND_DILATION) + strand_flip(transposed_filter(strand_flip(second_activation_gradient), second_weight_taps, SECOND_DILATION))
    first_activation_gradient = back_one(hidden_gradient)[0].astype(jnp.bfloat16)
    second_weight_gradient = weight_gradient_total(hidden_state, second_activation_gradient, SECOND_DILATION) + weight_gradient_total(strand_flip(hidden_state), strand_flip(second_activation_gradient), SECOND_DILATION)
    first_weight_gradient = weight_gradient_total(nucleotide_features, first_activation_gradient, FIRST_DILATION) + weight_gradient_total(strand_flip(nucleotide_features), strand_flip(first_activation_gradient), FIRST_DILATION)
    return (block_out, first_weight_gradient, second_weight_gradient)

def reference(codes, embed, first_weight_taps, second_weight_taps, cotangent):

    def step(pair):
        return one_window(pair[0], pair[1], embed, first_weight_taps, second_weight_taps)
    block_out, first_weight_gradient, second_weight_gradient = lax.map(step, (codes, cotangent))
    return (block_out, lax.optimization_barrier(jnp.sum(first_weight_gradient, axis=0)), lax.optimization_barrier(jnp.sum(second_weight_gradient, axis=0)))
```

```python
import functools

import jax
import jax.numpy as jnp
from jax import lax
from jax.experimental import pallas as pl
from jax.experimental.pallas import tpu as pltpu
from jax.sharding import PartitionSpec as P

FIRST_DILATION = 4
SECOND_DILATION = 16
LANES = 128
TILE = 256
BASES = 4
NONE = 4
BF16 = jnp.bfloat16
F32 = jnp.float32
MESH = pl.DeviceIdType.MESH
VMEM = pl.BlockSpec(memory_space=pltpu.VMEM)
ANY = pl.BlockSpec(memory_space=pl.ANY)
GELU_A = 0.7978845608028654
GELU_B = 0.044715


def dot(a, b):
    return jnp.dot(a, b, preferred_element_type=F32)


def dot_rows(a, b):
    return lax.dot_general(a, b, (((0,), (0,)), ((), ())), preferred_element_type=F32)


def flip_matrix(n):
    row = lax.broadcasted_iota(jnp.int32, (n, n), 0)
    col = lax.broadcasted_iota(jnp.int32, (n, n), 1)
    return (row + col == n - 1).astype(F32).astype(BF16)


def gelu_pair(x):
    square = x * x
    t = jnp.tanh(x * (GELU_A + (GELU_A * GELU_B) * square))
    half = 0.5 + 0.5 * t
    slope = GELU_A + (3.0 * GELU_A * GELU_B) * square
    return x * half, half + (0.5 * x) * (1.0 - t * t) * slope


def halo_kernel(count, codes_ref, cot_ref, ext_ref, halo_ref, code_in, cot_in, send, recv):
    me = lax.axis_index("seq")
    right, left = lax.rem(me + 1, count), lax.rem(me + count - 1, count)
    barrier = pltpu.get_barrier_semaphore()
    for peer in (left, right):
        pl.semaphore_signal(barrier, inc=1, device_id={"seq": peer}, device_id_type=MESH)
    pl.semaphore_wait(barrier, 2)
    length = codes_ref.shape[1]
    wide = SECOND_DILATION
    copies = []
    for i, (src, dst, peer) in enumerate(
        (
            (codes_ref.at[:, pl.ds(length - LANES, LANES)], code_in.at[0], right),
            (codes_ref.at[:, pl.ds(0, LANES)], code_in.at[1], left),
            (cot_ref.at[0, pl.ds(length - wide, wide)], cot_in.at[0], right),
            (cot_ref.at[0, pl.ds(0, wide)], cot_in.at[1], left),
        )
    ):
        copy = pltpu.make_async_remote_copy(
            src_ref=src,
            dst_ref=dst,
            send_sem=send.at[i],
            recv_sem=recv.at[i],
            device_id={"seq": peer},
            device_id_type=MESH,
        )
        copy.start()
        copies.append(copy)
    ext_ref[:, LANES : LANES + length] = codes_ref[...]
    for copy in copies:
        copy.wait()
    first, last = me == 0, me == count - 1
    ext_ref[:, :LANES] = jnp.where(first, NONE, code_in[0])
    ext_ref[:, LANES + length :] = jnp.where(last, NONE, code_in[1])
    zero = jnp.zeros((), BF16)
    halo_ref[:wide] = jnp.where(first, zero, cot_in[0])
    halo_ref[wide:] = jnp.where(last, zero, cot_in[1])


def exchange_halos(codes, cot):
    length, channels = cot.shape[1:]
    return pl.pallas_call(
        functools.partial(halo_kernel, lax.axis_size("seq")),
        out_shape=(
            jax.ShapeDtypeStruct((1, length + 2 * LANES), jnp.int32),
            jax.ShapeDtypeStruct((2 * SECOND_DILATION, channels), BF16),
        ),
        in_specs=[VMEM, ANY],
        out_specs=(VMEM, VMEM),
        scratch_shapes=[
            pltpu.VMEM((2, 1, LANES), jnp.int32),
            pltpu.VMEM((2, SECOND_DILATION, channels), BF16),
            pltpu.SemaphoreType.DMA((4,)),
            pltpu.SemaphoreType.DMA((4,)),
        ],
        compiler_params=pltpu.CompilerParams(collective_id=0, has_side_effects=True),
        name="halos",
    )(codes, cot)


def panel_kernel(
    ext_ref, halo_ref, cot_ref, embed_ref, first_ref, second_ref,
    block_ref, sums_ref,
    onehot, hidden, slope_one, grad_two, weight, weight_t, total,
):
    length, channels = cot_ref.shape[1:]
    wide = SECOND_DILATION
    span = ext_ref.shape[1]
    flip = flip_matrix(channels)

    def flipped(x):
        return dot(dot(flip, x).astype(BF16), flip)

    embed = embed_ref[...]
    table = jnp.zeros((16, channels), F32)
    for k in range(3):
        pair = second_ref[k].astype(F32) + flipped(second_ref[2 - k])
        weight[k] = pair.astype(BF16)
        weight_t[k] = pair.T.astype(BF16)
        row = lax.broadcasted_iota(jnp.int32, (16, BASES), 0)
        col = lax.broadcasted_iota(jnp.int32, (16, BASES), 1)
        place = (row == BASES * k + col).astype(F32).astype(BF16)
        rows = dot(place, embed).astype(BF16)
        table = table + dot(rows, first_ref[k])
        table = table + dot(rows, flipped(first_ref[2 - k]).astype(BF16))
    high = table.astype(BF16)
    rest = table - high.astype(F32)
    middle = rest.astype(BF16)
    low = (rest - middle.astype(F32)).astype(BF16)
    table = jnp.concatenate([high, middle, low], axis=0)

    codes = jnp.broadcast_to(ext_ref[...], (16, span))
    row = lax.broadcasted_iota(jnp.int32, (16, span), 0)
    before = pltpu.roll(codes, FIRST_DILATION, 1)
    after = pltpu.roll(codes, span - FIRST_DILATION, 1)
    tap = row // BASES
    seen = jnp.where(tap == 0, before, jnp.where(tap == 1, codes, after))
    hit = (seen == row % BASES) & (codes < NONE) & (row < 3 * BASES)
    hit = hit.astype(F32).astype(BF16)
    for part in range(3):
        onehot[16 * part : 16 * part + 16] = hit

    for start in range(0, span, TILE):
        size = min(TILE, span - start)
        pre = dot_rows(onehot[:, start : start + size], table)
        value, slope = gelu_pair(pre)
        hidden[start : start + size] = value.astype(BF16)
        slope_one[start : start + size] = slope

    def layer_two(start, size, cot):
        at = LANES + start
        pre = dot(hidden[at - wide : at - wide + size], weight[0])
        pre = pre + dot(hidden[at : at + size], weight[1])
        pre = pre + dot(hidden[at + wide : at + wide + size], weight[2])
        value, slope = gelu_pair(pre)
        grad_two[start + wide : start + wide + size] = (cot.astype(F32) * slope).astype(BF16)
        return value

    layer_two(-wide, wide, halo_ref[:wide])
    layer_two(length, wide, halo_ref[wide:])
    for start in range(0, length, TILE):
        value = layer_two(start, TILE, cot_ref[0, start : start + TILE])
        value = hidden[LANES + start : LANES + start + TILE].astype(F32) + value
        block_ref[0, start : start + TILE] = value.astype(BF16)

    sums = jnp.zeros((16, channels), F32)
    for start in range(0, length, TILE):
        at = LANES + start
        ahead, here, behind = (
            grad_two[start + shift : start + shift + TILE] for shift in (2 * wide, wide, 0)
        )
        value = hidden[at : at + TILE].T
        for k, grad in enumerate((ahead, here, behind)):
            term = dot(value, grad)
            total[k] = term if start == 0 else total[k] + term
        back = dot(ahead, weight_t[0]) + dot(here, weight_t[1]) + dot(behind, weight_t[2])
        back = back + cot_ref[0, start : start + TILE].astype(F32)
        grad_one = (back * slope_one[at : at + TILE]).astype(BF16)
        sums = sums + dot(onehot[:16, at : at + TILE], grad_one)

    def flipped_wide(x, rows):
        high = x.astype(BF16)
        low = (x - high.astype(F32)).astype(BF16)
        left = flip[:rows]
        return dot(dot(left, high).astype(BF16), flip) + dot(dot(left, low).astype(BF16), flip)

    half = channels // 2
    sums_ref[:channels] = (total[0] + flipped_wide(total[2], channels)).astype(BF16)
    sums_ref[channels : channels + half] = (total[1, :half] + flipped_wide(total[1], half)).astype(BF16)
    sums_ref[channels + half : channels + half + 16] = sums.astype(BF16)
    left_over = sums_ref.shape[0] - (channels + half + 16)
    if left_over:
        sums_ref[channels + half + 16 :] = jnp.zeros((left_over, channels), BF16)


def panel(ext, halo, cot, embed, first, second, rows):
    length, channels = cot.shape[1:]
    span = ext.shape[1]
    return pl.pallas_call(
        panel_kernel,
        out_shape=(
            jax.ShapeDtypeStruct(cot.shape, BF16),
            jax.ShapeDtypeStruct((rows, channels), BF16),
        ),
        in_specs=[VMEM] * 6,
        out_specs=(VMEM, VMEM),
        scratch_shapes=[
            pltpu.VMEM((48, span), BF16),
            pltpu.VMEM((span, channels), BF16),
            pltpu.VMEM((span, channels), F32),
            pltpu.VMEM((length + 2 * SECOND_DILATION, channels), BF16),
            pltpu.VMEM((3, channels, channels), BF16),
            pltpu.VMEM((3, channels, channels), BF16),
            pltpu.VMEM((3, channels, channels), F32),
        ],
        compiler_params=pltpu.CompilerParams(vmem_limit_bytes=40 * 1024 * 1024),
        name="panel",
    )(ext, halo, cot, embed, first, second)


def reduce_kernel(across, along, x_ref, o_ref, in_seq, part, in_dp, held, *sems):
    d, q = lax.axis_index("dp"), lax.axis_index("seq")
    barrier = pltpu.get_barrier_semaphore()
    seq_peers = [lax.rem(q + o, along) for o in range(1, along)]
    dp_peers = [lax.rem(d + o, across) for o in range(1, across)]
    for peer in seq_peers:
        pl.semaphore_signal(barrier, inc=1, device_id={"seq": peer}, device_id_type=MESH)
    for peer in dp_peers:
        pl.semaphore_signal(barrier, inc=1, device_id={"dp": peer}, device_id_type=MESH)
    pl.semaphore_wait(barrier, along + across - 2)

    def start(axis, phase, i, peer, src, dst):
        copy = pltpu.make_async_remote_copy(
            src_ref=src,
            dst_ref=dst,
            send_sem=sems[2 * phase].at[i],
            recv_sem=sems[2 * phase + 1].at[i],
            device_id={axis: peer},
            device_id_type=MESH,
        )
        copy.start()
        return copy

    def wait_all(copies):
        for copy in copies:
            copy.wait_recv()
        for copy in copies:
            copy.wait_send()

    copies = [
        start("seq", 0, i, peer, x_ref.at[peer], in_seq.at[i]) for i, peer in enumerate(seq_peers)
    ]
    wait_all(copies)
    value = x_ref[q].astype(F32)
    for i in range(along - 1):
        value = value + in_seq[i].astype(F32)
    part[...] = value.astype(BF16)

    copies = [start("dp", 1, i, peer, part.at[peer], in_dp.at[i]) for i, peer in enumerate(dp_peers)]
    wait_all(copies)
    value = part[d].astype(F32)
    for i in range(across - 1):
        value = value + in_dp[i].astype(F32)
    held[q, d] = value.astype(BF16)

    mine = held.at[q, d]
    copies = [start("dp", 2, i, peer, mine, mine) for i, peer in enumerate(dp_peers)]
    wait_all(copies)
    mine = held.at[q]
    copies = [start("seq", 3, i, peer, mine, mine) for i, peer in enumerate(seq_peers)]
    wait_all(copies)
    o_ref[...] = held[...]


def reduce_sums(x):
    along, across, rows, channels = x.shape
    sems = []
    for count in (along, across, across, along):
        sems += [pltpu.SemaphoreType.DMA((count - 1,))] * 2
    return pl.pallas_call(
        functools.partial(reduce_kernel, across, along),
        out_shape=jax.ShapeDtypeStruct(x.shape, BF16),
        in_specs=[VMEM],
        out_specs=VMEM,
        scratch_shapes=[
            pltpu.VMEM((along - 1, across, rows, channels), BF16),
            pltpu.VMEM((across, rows, channels), BF16),
            pltpu.VMEM((across - 1, rows, channels), BF16),
            pltpu.VMEM(x.shape, BF16),
            *sems,
        ],
        compiler_params=pltpu.CompilerParams(
            collective_id=1, has_side_effects=True, vmem_limit_bytes=40 * 1024 * 1024
        ),
        name="sums",
    )(x)


def expand_kernel(x_ref, embed_ref, first_ref, second_ref):
    channels = embed_ref.shape[1]
    half = channels // 2
    flip = flip_matrix(channels)
    outer = x_ref[:channels]
    second_ref[0] = outer.astype(F32)
    second_ref[2] = dot(dot(flip, outer).astype(BF16), flip)
    inner = x_ref[channels : channels + half]
    second_ref[1, :half] = inner.astype(F32)
    second_ref[1, half:] = dot(dot(flip[half:, :half], inner).astype(BF16), flip)
    sums = x_ref[channels + half : channels + half + 16]
    sums_flip = dot(sums, flip).astype(BF16)
    embed = embed_ref[...]
    for k in range(3):
        row = lax.broadcasted_iota(jnp.int32, (16, BASES), 0)
        col = lax.broadcasted_iota(jnp.int32, (16, BASES), 1)
        here = dot((row == BASES * k + col).astype(F32).astype(BF16), embed).astype(BF16)
        there = dot((row == BASES * (2 - k) + col).astype(F32).astype(BF16), embed).astype(BF16)
        there = dot(there, flip).astype(BF16)
        first_ref[k] = dot_rows(here, sums) + dot_rows(there, sums_flip)


def expand(x, embed):
    channels = x.shape[1]
    shape = jax.ShapeDtypeStruct((3, channels, channels), F32)
    return pl.pallas_call(
        expand_kernel,
        out_shape=(shape, shape),
        in_specs=[VMEM] * 2,
        out_specs=(VMEM, VMEM),
        compiler_params=pltpu.CompilerParams(vmem_limit_bytes=32 * 1024 * 1024),
        name="expand",
    )(x, embed)


def local(codes, embed, first, second, cot):
    channels = cot.shape[2]
    across, along = lax.axis_size("dp"), lax.axis_size("seq")
    devices = across * along
    needed = channels + channels // 2 + 16
    rows = 16 * pl.cdiv(needed, 16 * devices)
    ext, halo = exchange_halos(codes, cot)
    block_out, sums = panel(ext, halo, cot, embed, first, second, rows * devices)
    sums = reduce_sums(sums.reshape(along, across, rows, channels))
    first_grad, second_grad = expand(sums.reshape(rows * devices, channels), embed)
    return block_out, first_grad, second_grad


def solution(mesh):
    in_specs = (P("dp", "seq"), P(), P(), P(), P("dp", "seq", None))
    out_specs = (P("dp", "seq", None), P(), P())
    return jax.shard_map(local, mesh=mesh, in_specs=in_specs, out_specs=out_specs, check_vma=False)
```

```python
import functools

import jax
import jax.numpy as jnp
from jax import lax
from jax.experimental import pallas as pl
from jax.experimental.pallas import tpu as pltpu
from jax.sharding import PartitionSpec as P

FIRST_DILATION = 4
SECOND_DILATION = 16
LANES = 128
TILE = 256
BASES = 4
NONE = 4
BF16 = jnp.bfloat16
F32 = jnp.float32
MESH = pl.DeviceIdType.MESH
UNROLL = 8
VMEM = pl.BlockSpec(memory_space=pltpu.VMEM)
ANY = pl.BlockSpec(memory_space=pl.ANY)
GELU_A = 0.7978845608028654
GELU_B = 0.044715


def dot(a, b):
    return jnp.dot(a, b, preferred_element_type=F32)


def dot_rows(a, b):
    return lax.dot_general(a, b, (((0,), (0,)), ((), ())), preferred_element_type=F32)


def flip_matrix(n):
    row = lax.broadcasted_iota(jnp.int32, (n, n), 0)
    col = lax.broadcasted_iota(jnp.int32, (n, n), 1)
    return (row + col == n - 1).astype(F32).astype(BF16)


def gelu_pair(x):
    square = x * x
    t = jnp.tanh(x * (GELU_A + (GELU_A * GELU_B) * square))
    half = 0.5 + 0.5 * t
    slope = GELU_A + (3.0 * GELU_A * GELU_B) * square
    return x * half, half + (0.5 * x) * (1.0 - t * t) * slope


def panel_kernel(
    across, along, blocks,
    codes_ref, cot_ref, embed_ref, first_ref, second_ref,
    block_ref, rows_ref, sums_ref,
    ext, cot, first, second, code_in, cot_in, onehot, hidden, slope_one, grad_two,
    weight, weight_t, total, acc, mine, own_sum, in_seq, in_sum, part, in_dp, held, block,
    load, halo_send, halo_recv, *sems,
):
    d, q = lax.axis_index("dp"), lax.axis_index("seq")
    seq_peers = [lax.rem(q + o, along) for o in range(1, along)]
    dp_peers = [lax.rem(d + o, across) for o in range(1, across)]
    right, left = seq_peers[0], seq_peers[-1]
    length, channels = cot_ref.shape[1:]
    half = channels // 2
    wide = SECOND_DILATION
    span = ext.shape[1]
    tiles = length // TILE

    loads = [
        pltpu.make_async_copy(src, dst, load.at[i])
        for i, (src, dst) in enumerate(
            (
                (second_ref, second),
                (first_ref, first),
                (codes_ref, ext.at[:, pl.ds(LANES, length)]),
                (cot_ref, cot),
            )
        )
    ]
    for copy in loads:
        copy.start()

    barrier = pltpu.get_barrier_semaphore()
    for peer in seq_peers:
        pl.semaphore_signal(barrier, inc=1, device_id={"seq": peer}, device_id_type=MESH)
    for peer in dp_peers:
        pl.semaphore_signal(barrier, inc=1, device_id={"dp": peer}, device_id_type=MESH)

    def send(axis, peer, src, dst, send_sem, recv_sem):
        copy = pltpu.make_async_remote_copy(
            src_ref=src,
            dst_ref=dst,
            send_sem=send_sem,
            recv_sem=recv_sem,
            device_id={axis: peer},
            device_id_type=MESH,
        )
        copy.start()
        return copy

    def send_all(axis, peers, phase, src, dst):
        out, into = sems[2 * phase], sems[2 * phase + 1]
        return [
            send(axis, peer, src(peer), dst(i), out.at[i], into.at[i])
            for i, peer in enumerate(peers)
        ]

    flip = flip_matrix(channels)

    def flipped(x):
        return dot(dot(flip, x).astype(BF16), flip)

    embed = embed_ref[...]
    loads[0].wait()
    for k in range(3):
        pair = second[k].astype(F32) + flipped(second[2 - k])
        weight[k] = pair.astype(BF16)
        weight_t[k] = pair.T.astype(BF16)
    loads[1].wait()
    table = jnp.zeros((16, channels), F32)
    for k in range(3):
        row = lax.broadcasted_iota(jnp.int32, (16, BASES), 0)
        col = lax.broadcasted_iota(jnp.int32, (16, BASES), 1)
        place = (row == BASES * k + col).astype(F32).astype(BF16)
        rows = dot(place, embed).astype(BF16)
        table = table + dot(rows, first[k])
        table = table + dot(rows, flipped(first[2 - k]).astype(BF16))
    high = table.astype(BF16)
    rest = table - high.astype(F32)
    middle = rest.astype(BF16)
    low = (rest - middle.astype(F32)).astype(BF16)
    table = jnp.concatenate([high, middle, low], axis=0)

    pl.semaphore_wait(barrier, along + across - 2)
    halos = [
        send(axis, peer, src, dst, halo_send.at[i], halo_recv.at[i])
        for i, (axis, peer, src, dst) in enumerate(
            (
                ("seq", right, codes_ref.at[:, pl.ds(length - LANES, LANES)], code_in.at[0]),
                ("seq", left, codes_ref.at[:, pl.ds(0, LANES)], code_in.at[1]),
                ("seq", right, cot_ref.at[0, pl.ds(length - wide, wide)], cot_in.at[0]),
                ("seq", left, cot_ref.at[0, pl.ds(0, wide)], cot_in.at[1]),
            )
        )
    ]

    def fill_onehot():
        codes = jnp.broadcast_to(ext[...], (16, span))
        row = lax.broadcasted_iota(jnp.int32, (16, span), 0)
        before = pltpu.roll(codes, FIRST_DILATION, 1)
        after = pltpu.roll(codes, span - FIRST_DILATION, 1)
        tap = row // BASES
        seen = jnp.where(tap == 0, before, jnp.where(tap == 1, codes, after))
        hit = (seen == row % BASES) & (codes < NONE) & (row < 3 * BASES)
        hit = hit.astype(F32).astype(BF16)
        for copy in range(3):
            onehot[16 * copy : 16 * copy + 16] = hit

    def at(start, size):
        return pl.ds(pl.multiple_of(start, wide), size)

    def layer_one(start, size):
        place = pl.ds(pl.multiple_of(start, LANES), size)
        value, slope = gelu_pair(dot_rows(onehot[:, place], table))
        hidden[place] = value.astype(BF16)
        slope_one[place] = slope

    def layer_two(start, size, grad):
        pre = dot(hidden[at(start + LANES - wide, size)], weight[0])
        pre = pre + dot(hidden[at(start + LANES, size)], weight[1])
        pre = pre + dot(hidden[at(start + LANES + wide, size)], weight[2])
        value, slope = gelu_pair(pre)
        grad_two[at(start + wide, size)] = (grad.astype(F32) * slope).astype(BF16)
        return value

    def tile_one(i):
        layer_one(i * TILE + LANES, TILE)

    def tile_two(i):
        start = i * TILE
        value = layer_two(start, TILE, cot[0, at(start, TILE)])
        value = hidden[at(start + LANES, TILE)].astype(F32) + value
        block[0, at(start, TILE)] = value.astype(BF16)

    def loop(first, last, body):
        if last > first:
            lax.fori_loop(first, last, lambda i, c: (body(i), c)[1], 0, unroll=min(UNROLL, last - first))

    ext[:, :LANES] = jnp.full((1, LANES), NONE, jnp.int32)
    ext[:, LANES + length :] = jnp.full((1, LANES), NONE, jnp.int32)
    loads[2].wait()
    fill_onehot()
    loop(1, tiles - 1, tile_one)
    loads[3].wait()
    loop(2, tiles - 2, tile_two)

    for copy in halos:
        copy.wait()
    at_first, at_last = q == 0, q == along - 1
    ext[:, :LANES] = jnp.where(at_first, NONE, code_in[0])
    ext[:, LANES + length :] = jnp.where(at_last, NONE, code_in[1])
    fill_onehot()
    layer_one(0, LANES + TILE)
    layer_one(span - LANES - TILE, LANES + TILE)
    zero = jnp.zeros((), BF16)
    layer_two(-wide, wide, jnp.where(at_first, zero, cot_in[0]))
    layer_two(length, wide, jnp.where(at_last, zero, cot_in[1]))
    for i in (0, 1, tiles - 2, tiles - 1):
        tile_two(i)

    stored = pltpu.make_async_copy(block, block_ref, load.at[4])
    stored.start()

    total[...] = jnp.zeros_like(total)

    def tile_terms(i):
        start = i * TILE
        value = hidden[at(start + LANES, TILE)].T
        for k in range(3):
            total[k] += dot(value, grad_two[at(start + (2 - k) * wide, TILE)])

    loop(0, tiles, tile_terms)

    def flipped_wide(x, rows):
        high = x.astype(BF16)
        low = (x - high.astype(F32)).astype(BF16)
        left = flip[:rows]
        return dot(dot(left, high).astype(BF16), flip) + dot(dot(left, low).astype(BF16), flip)

    outer = (total[0] + flipped_wide(total[2], channels)).astype(BF16)
    inner = (total[1, :half] + flipped_wide(total[1], half)).astype(BF16)
    filled = (channels + half) // 16
    for b in range(along * blocks):
        if 16 * b < channels:
            value = outer[16 * b : 16 * b + 16]
        elif b < filled:
            value = inner[16 * b - channels : 16 * b - channels + 16]
        else:
            value = jnp.zeros((16, channels), BF16)
        mine[b // blocks, b % blocks] = value

    first_copies = send_all("seq", seq_peers, 0, lambda peer: mine.at[peer], lambda i: in_seq.at[i])

    acc[...] = jnp.zeros_like(acc)

    def tile_back(i):
        start = i * TILE
        back = cot[0, at(start, TILE)].astype(F32)
        for k in range(3):
            back = back + dot(grad_two[at(start + (2 - k) * wide, TILE)], weight_t[k])
        grad = (back * slope_one[at(start + LANES, TILE)]).astype(BF16)
        acc[...] += dot(onehot[:16, pl.ds(pl.multiple_of(start + LANES, LANES), TILE)], grad)

    loop(0, tiles, tile_back)
    own_sum[...] = acc[...].astype(BF16)
    to_sum = in_sum.at[q]
    sum_copies = send_all("seq", seq_peers, 1, lambda peer: own_sum, lambda i: to_sum)
    in_sum[q] = own_sum[...]

    for copy in first_copies:
        copy.wait()
    value = mine[q].astype(F32)
    for i in range(along - 1):
        value = value + in_seq[i].astype(F32)
    part[:blocks] = value.astype(BF16)
    if across > blocks + 1:
        part[blocks + 1 :] = jnp.zeros((across - blocks - 1, 16, channels), BF16)
    for copy in sum_copies:
        copy.wait()
    value = in_sum[0].astype(F32)
    for i in range(1, along):
        value = value + in_sum[i].astype(F32)
    part[blocks] = value.astype(BF16)

    copies = send_all("dp", dp_peers, 2, lambda peer: part.at[peer], lambda i: in_dp.at[i])
    for copy in copies:
        copy.wait()
    value = part[d].astype(F32)
    for i in range(across - 1):
        value = value + in_dp[i].astype(F32)
    held[q, d] = value.astype(BF16)

    ready = held.at[q, d]
    copies = send_all("dp", dp_peers, 3, lambda peer: ready, lambda i: ready)
    for copy in copies:
        copy.wait()
    group = held.at[q, pl.ds(0, blocks)]
    copies = send_all("seq", seq_peers, 4, lambda peer: group, lambda i: group)
    for copy in copies:
        copy.wait()
    for i in range(along):
        rows_ref[i] = held[i, :blocks]
    sums_ref[...] = held[q, blocks]
    stored.wait()


def panel(codes, embed, first, second, cot):
    length, channels = cot.shape[1:]
    span = length + 2 * LANES
    across, along = lax.axis_size("dp"), lax.axis_size("seq")
    blocks = pl.cdiv(channels + channels // 2, 16 * along)
    assert blocks < across and length % TILE == 0 and length // TILE >= 4
    sems = []
    for count in (along, along, across, across, along):
        sems += [pltpu.SemaphoreType.DMA((count - 1,))] * 2
    return pl.pallas_call(
        functools.partial(panel_kernel, across, along, blocks),
        out_shape=(
            jax.ShapeDtypeStruct(cot.shape, BF16),
            jax.ShapeDtypeStruct((along, blocks, 16, channels), BF16),
            jax.ShapeDtypeStruct((16, channels), BF16),
        ),
        in_specs=[ANY, ANY, VMEM, ANY, ANY],
        out_specs=(ANY, VMEM, VMEM),
        scratch_shapes=[
            pltpu.VMEM((1, span), jnp.int32),
            pltpu.VMEM(cot.shape, BF16),
            pltpu.VMEM(first.shape, BF16),
            pltpu.VMEM(second.shape, BF16),
            pltpu.VMEM((2, 1, LANES), jnp.int32),
            pltpu.VMEM((2, SECOND_DILATION, channels), BF16),
            pltpu.VMEM((48, span), BF16),
            pltpu.VMEM((span, channels), BF16),
            pltpu.VMEM((span, channels), F32),
            pltpu.VMEM((length + 2 * SECOND_DILATION, channels), BF16),
            pltpu.VMEM((3, channels, channels), BF16),
            pltpu.VMEM((3, channels, channels), BF16),
            pltpu.VMEM((3, channels, channels), F32),
            pltpu.VMEM((16, channels), F32),
            pltpu.VMEM((along, blocks, 16, channels), BF16),
            pltpu.VMEM((16, channels), BF16),
            pltpu.VMEM((along - 1, blocks, 16, channels), BF16),
            pltpu.VMEM((along, 16, channels), BF16),
            pltpu.VMEM((across, 16, channels), BF16),
            pltpu.VMEM((across - 1, 16, channels), BF16),
            pltpu.VMEM((along, across, 16, channels), BF16),
            pltpu.VMEM(cot.shape, BF16),
            pltpu.SemaphoreType.DMA((5,)),
            pltpu.SemaphoreType.DMA((4,)),
            pltpu.SemaphoreType.DMA((4,)),
            *sems,
        ],
        compiler_params=pltpu.CompilerParams(
            collective_id=0, has_side_effects=True, vmem_limit_bytes=60 * 1024 * 1024
        ),
        name="panel",
    )(codes, cot, embed, first, second)


def expand_kernel(x_ref, sums_ref, embed_ref, block_ref, out_ref, first_ref, second_ref, block, done):
    fetch = pltpu.make_async_copy(block_ref, block, done.at[0])
    fetch.start()
    channels = embed_ref.shape[1]
    half = channels // 2
    flip = flip_matrix(channels)
    outer = x_ref[:channels]
    second_ref[0] = outer.astype(F32)
    second_ref[2] = dot(dot(flip, outer).astype(BF16), flip)
    inner = x_ref[channels : channels + half]
    second_ref[1, :half] = inner.astype(F32)
    second_ref[1, half:] = dot(dot(flip[half:, :half], inner).astype(BF16), flip)
    fetch.wait()
    move = pltpu.make_async_copy(block, out_ref, done.at[1])
    move.start()
    sums = sums_ref[...]
    sums_flip = dot(sums, flip).astype(BF16)
    embed = embed_ref[...]
    for k in range(3):
        row = lax.broadcasted_iota(jnp.int32, (16, BASES), 0)
        col = lax.broadcasted_iota(jnp.int32, (16, BASES), 1)
        here = dot((row == BASES * k + col).astype(F32).astype(BF16), embed).astype(BF16)
        there = dot((row == BASES * (2 - k) + col).astype(F32).astype(BF16), embed).astype(BF16)
        there = dot(there, flip).astype(BF16)
        first_ref[k] = dot_rows(here, sums) + dot_rows(there, sums_flip)
    move.wait()


def expand(x, sums, embed, block):
    channels = x.shape[1]
    shape = jax.ShapeDtypeStruct((3, channels, channels), F32)
    return pl.pallas_call(
        expand_kernel,
        out_shape=(jax.ShapeDtypeStruct(block.shape, BF16), shape, shape),
        in_specs=[VMEM, VMEM, VMEM, ANY],
        out_specs=(ANY, VMEM, VMEM),
        scratch_shapes=[pltpu.VMEM(block.shape, BF16), pltpu.SemaphoreType.DMA((2,))],
        compiler_params=pltpu.CompilerParams(vmem_limit_bytes=60 * 1024 * 1024),
        name="expand",
    )(x, sums, embed, block)


def local(codes, embed, first, second, cot):
    block, rows, sums = panel(codes, embed, first, second, cot)
    return expand(rows.reshape(-1, cot.shape[2]), sums, embed, block)


def solution(mesh):
    in_specs = (P("dp", "seq"), P(), P(), P(), P("dp", "seq", None))
    out_specs = (P("dp", "seq", None), P(), P())
    return jax.shard_map(local, mesh=mesh, in_specs=in_specs, out_specs=out_specs, check_vma=False)
```

```python
import functools

import jax
import jax.numpy as jnp
from jax import lax
from jax.experimental import pallas as pl
from jax.experimental.pallas import tpu as pltpu
from jax.sharding import PartitionSpec as P

FIRST_DILATION = 4
SECOND_DILATION = 16
LANES = 128
TILE = 256
BASES = 4
NONE = 4
BF16 = jnp.bfloat16
F32 = jnp.float32
MESH = pl.DeviceIdType.MESH
UNROLL = 8
VMEM = pl.BlockSpec(memory_space=pltpu.VMEM)
ANY = pl.BlockSpec(memory_space=pl.ANY)
GELU_A = 0.7978845608028654
GELU_B = 0.044715


def dot(a, b):
    return jnp.dot(a, b, preferred_element_type=F32)


def dot_rows(a, b):
    return lax.dot_general(a, b, (((0,), (0,)), ((), ())), preferred_element_type=F32)


def flip_matrix(n):
    row = lax.broadcasted_iota(jnp.int32, (n, n), 0)
    col = lax.broadcasted_iota(jnp.int32, (n, n), 1)
    return (row + col == n - 1).astype(F32).astype(BF16)


def gelu_pair(x):
    square = x * x
    t = jnp.tanh(x * (GELU_A + (GELU_A * GELU_B) * square))
    half = 0.5 + 0.5 * t
    slope = GELU_A + (3.0 * GELU_A * GELU_B) * square
    return x * half, half + (0.5 * x) * (1.0 - t * t) * slope


def panel_kernel(
    across, along, blocks,
    codes_ref, cot_ref, embed_ref, first_ref, second_ref,
    block_ref, rows_ref, sums_ref,
    ext, cot, first, second, code_in, cot_in, onehot, hidden, slope_one, grad_two,
    weight, weight_t, total, acc, mine, own_sum, in_seq, in_sum, part, in_dp, held,
    load, halo_send, halo_recv, *sems,
):
    d, q = lax.axis_index("dp"), lax.axis_index("seq")
    seq_peers = [lax.rem(q + o, along) for o in range(1, along)]
    dp_peers = [lax.rem(d + o, across) for o in range(1, across)]
    right, left = seq_peers[0], seq_peers[-1]
    length, channels = cot_ref.shape[1:]
    half = channels // 2
    wide = SECOND_DILATION
    span = ext.shape[1]
    tiles = length // TILE

    loads = [
        pltpu.make_async_copy(src, dst, load.at[i])
        for i, (src, dst) in enumerate(
            (
                (second_ref, second),
                (first_ref, first),
                (codes_ref, ext.at[:, pl.ds(LANES, length)]),
                (cot_ref, cot),
            )
        )
    ]
    for copy in loads:
        copy.start()

    barrier = pltpu.get_barrier_semaphore()
    for peer in seq_peers:
        pl.semaphore_signal(barrier, inc=1, device_id={"seq": peer}, device_id_type=MESH)
    for peer in dp_peers:
        pl.semaphore_signal(barrier, inc=1, device_id={"dp": peer}, device_id_type=MESH)

    def send(axis, peer, src, dst, send_sem, recv_sem):
        copy = pltpu.make_async_remote_copy(
            src_ref=src,
            dst_ref=dst,
            send_sem=send_sem,
            recv_sem=recv_sem,
            device_id={axis: peer},
            device_id_type=MESH,
        )
        copy.start()
        return copy

    def send_all(axis, peers, phase, src, dst):
        out, into = sems[2 * phase], sems[2 * phase + 1]
        return [
            send(axis, peer, src(peer), dst(i), out.at[i], into.at[i])
            for i, peer in enumerate(peers)
        ]

    flip = flip_matrix(channels)

    def flipped(x):
        return dot(dot(flip, x).astype(BF16), flip)

    embed = embed_ref[...]
    loads[0].wait()
    for k in range(3):
        pair = second[k].astype(F32) + flipped(second[2 - k])
        weight[k] = pair.astype(BF16)
        weight_t[k] = pair.T.astype(BF16)
    loads[1].wait()
    table = jnp.zeros((16, channels), F32)
    for k in range(3):
        row = lax.broadcasted_iota(jnp.int32, (16, BASES), 0)
        col = lax.broadcasted_iota(jnp.int32, (16, BASES), 1)
        place = (row == BASES * k + col).astype(F32).astype(BF16)
        rows = dot(place, embed).astype(BF16)
        table = table + dot(rows, first[k])
        table = table + dot(rows, flipped(first[2 - k]).astype(BF16))
    high = table.astype(BF16)
    rest = table - high.astype(F32)
    middle = rest.astype(BF16)
    low = (rest - middle.astype(F32)).astype(BF16)
    table = jnp.concatenate([high, middle, low], axis=0)

    pl.semaphore_wait(barrier, along + across - 2)
    halos = [
        send(axis, peer, src, dst, halo_send.at[i], halo_recv.at[i])
        for i, (axis, peer, src, dst) in enumerate(
            (
                ("seq", right, codes_ref.at[:, pl.ds(length - LANES, LANES)], code_in.at[0]),
                ("seq", left, codes_ref.at[:, pl.ds(0, LANES)], code_in.at[1]),
                ("seq", right, cot_ref.at[0, pl.ds(length - wide, wide)], cot_in.at[0]),
                ("seq", left, cot_ref.at[0, pl.ds(0, wide)], cot_in.at[1]),
            )
        )
    ]

    def fill_onehot():
        codes = jnp.broadcast_to(ext[...], (16, span))
        row = lax.broadcasted_iota(jnp.int32, (16, span), 0)
        before = pltpu.roll(codes, FIRST_DILATION, 1)
        after = pltpu.roll(codes, span - FIRST_DILATION, 1)
        tap = row // BASES
        seen = jnp.where(tap == 0, before, jnp.where(tap == 1, codes, after))
        hit = (seen == row % BASES) & (codes < NONE) & (row < 3 * BASES)
        hit = hit.astype(F32).astype(BF16)
        for copy in range(3):
            onehot[16 * copy : 16 * copy + 16] = hit

    def at(start, size):
        return pl.ds(pl.multiple_of(start, wide), size)

    def layer_one(start, size):
        place = pl.ds(pl.multiple_of(start, LANES), size)
        value, slope = gelu_pair(dot_rows(onehot[:, place], table))
        hidden[place] = value.astype(BF16)
        slope_one[place] = slope

    def layer_two(start, size, grad):
        pre = dot(hidden[at(start + LANES - wide, size)], weight[0])
        pre = pre + dot(hidden[at(start + LANES, size)], weight[1])
        pre = pre + dot(hidden[at(start + LANES + wide, size)], weight[2])
        value, slope = gelu_pair(pre)
        grad_two[at(start + wide, size)] = (grad.astype(F32) * slope).astype(BF16)
        return value

    def tile_one(i):
        layer_one(i * TILE + LANES, TILE)

    def tile_two(i):
        start = i * TILE
        value = layer_two(start, TILE, cot[0, at(start, TILE)])
        value = hidden[at(start + LANES, TILE)].astype(F32) + value
        block_ref[0, at(start, TILE)] = value.astype(BF16)

    def loop(first, last, body):
        if last > first:
            lax.fori_loop(first, last, lambda i, c: (body(i), c)[1], 0, unroll=min(UNROLL, last - first))

    ext[:, :LANES] = jnp.full((1, LANES), NONE, jnp.int32)
    ext[:, LANES + length :] = jnp.full((1, LANES), NONE, jnp.int32)
    loads[2].wait()
    fill_onehot()
    loop(1, tiles - 1, tile_one)
    loads[3].wait()
    loop(2, tiles - 2, tile_two)

    for copy in halos:
        copy.wait()
    at_first, at_last = q == 0, q == along - 1
    ext[:, :LANES] = jnp.where(at_first, NONE, code_in[0])
    ext[:, LANES + length :] = jnp.where(at_last, NONE, code_in[1])
    fill_onehot()
    layer_one(0, LANES + TILE)
    layer_one(span - LANES - TILE, LANES + TILE)
    zero = jnp.zeros((), BF16)
    layer_two(-wide, wide, jnp.where(at_first, zero, cot_in[0]))
    layer_two(length, wide, jnp.where(at_last, zero, cot_in[1]))
    for i in (0, 1, tiles - 2, tiles - 1):
        tile_two(i)

    total[...] = jnp.zeros_like(total)

    def tile_terms(i):
        start = i * TILE
        value = hidden[at(start + LANES, TILE)].T
        for k in range(3):
            total[k] += dot(value, grad_two[at(start + (2 - k) * wide, TILE)])

    loop(0, tiles, tile_terms)

    def flipped_wide(x, rows):
        high = x.astype(BF16)
        low = (x - high.astype(F32)).astype(BF16)
        left = flip[:rows]
        return dot(dot(left, high).astype(BF16), flip) + dot(dot(left, low).astype(BF16), flip)

    outer = (total[0] + flipped_wide(total[2], channels)).astype(BF16)
    inner = (total[1, :half] + flipped_wide(total[1], half)).astype(BF16)
    filled = (channels + half) // 16
    for b in range(along * blocks):
        if 16 * b < channels:
            value = outer[16 * b : 16 * b + 16]
        elif b < filled:
            value = inner[16 * b - channels : 16 * b - channels + 16]
        else:
            value = jnp.zeros((16, channels), BF16)
        mine[b // blocks, b % blocks] = value

    first_copies = send_all("seq", seq_peers, 0, lambda peer: mine.at[peer], lambda i: in_seq.at[i])

    acc[...] = jnp.zeros_like(acc)

    def tile_back(i):
        start = i * TILE
        back = cot[0, at(start, TILE)].astype(F32)
        for k in range(3):
            back = back + dot(grad_two[at(start + (2 - k) * wide, TILE)], weight_t[k])
        grad = (back * slope_one[at(start + LANES, TILE)]).astype(BF16)
        acc[...] += dot(onehot[:16, pl.ds(pl.multiple_of(start + LANES, LANES), TILE)], grad)

    loop(0, tiles, tile_back)
    own_sum[...] = acc[...].astype(BF16)
    to_sum = in_sum.at[q]
    sum_copies = send_all("seq", seq_peers, 1, lambda peer: own_sum, lambda i: to_sum)
    in_sum[q] = own_sum[...]

    for copy in first_copies:
        copy.wait()
    value = mine[q].astype(F32)
    for i in range(along - 1):
        value = value + in_seq[i].astype(F32)
    part[:blocks] = value.astype(BF16)
    if across > blocks + 1:
        part[blocks + 1 :] = jnp.zeros((across - blocks - 1, 16, channels), BF16)
    for copy in sum_copies:
        copy.wait()
    value = in_sum[0].astype(F32)
    for i in range(1, along):
        value = value + in_sum[i].astype(F32)
    part[blocks] = value.astype(BF16)

    copies = send_all("dp", dp_peers, 2, lambda peer: part.at[peer], lambda i: in_dp.at[i])
    for copy in copies:
        copy.wait()
    value = part[d].astype(F32)
    for i in range(across - 1):
        value = value + in_dp[i].astype(F32)
    held[q, d] = value.astype(BF16)

    ready = held.at[q, d]
    copies = send_all("dp", dp_peers, 3, lambda peer: ready, lambda i: ready)
    for copy in copies:
        copy.wait()
    group = held.at[q, pl.ds(0, blocks)]
    copies = send_all("seq", seq_peers, 4, lambda peer: group, lambda i: group)
    for copy in copies:
        copy.wait()
    for i in range(along):
        rows_ref[i] = held[i, :blocks]
    sums_ref[...] = held[q, blocks]


def panel(codes, embed, first, second, cot):
    length, channels = cot.shape[1:]
    span = length + 2 * LANES
    across, along = lax.axis_size("dp"), lax.axis_size("seq")
    blocks = pl.cdiv(channels + channels // 2, 16 * along)
    assert blocks < across and length % TILE == 0 and length // TILE >= 4
    sems = []
    for count in (along, along, across, across, along):
        sems += [pltpu.SemaphoreType.DMA((count - 1,))] * 2
    return pl.pallas_call(
        functools.partial(panel_kernel, across, along, blocks),
        out_shape=(
            pltpu.VMEM(cot.shape, BF16),
            pltpu.VMEM((along, blocks, 16, channels), BF16),
            pltpu.VMEM((16, channels), BF16),
        ),
        in_specs=[ANY, ANY, VMEM, ANY, ANY],
        out_specs=(VMEM, VMEM, VMEM),
        scratch_shapes=[
            pltpu.VMEM((1, span), jnp.int32),
            pltpu.VMEM(cot.shape, BF16),
            pltpu.VMEM(first.shape, BF16),
            pltpu.VMEM(second.shape, BF16),
            pltpu.VMEM((2, 1, LANES), jnp.int32),
            pltpu.VMEM((2, SECOND_DILATION, channels), BF16),
            pltpu.VMEM((48, span), BF16),
            pltpu.VMEM((span, channels), BF16),
            pltpu.VMEM((span, channels), F32),
            pltpu.VMEM((length + 2 * SECOND_DILATION, channels), BF16),
            pltpu.VMEM((3, channels, channels), BF16),
            pltpu.VMEM((3, channels, channels), BF16),
            pltpu.VMEM((3, channels, channels), F32),
            pltpu.VMEM((16, channels), F32),
            pltpu.VMEM((along, blocks, 16, channels), BF16),
            pltpu.VMEM((16, channels), BF16),
            pltpu.VMEM((along - 1, blocks, 16, channels), BF16),
            pltpu.VMEM((along, 16, channels), BF16),
            pltpu.VMEM((across, 16, channels), BF16),
            pltpu.VMEM((across - 1, 16, channels), BF16),
            pltpu.VMEM((along, across, 16, channels), BF16),
            pltpu.SemaphoreType.DMA((4,)),
            pltpu.SemaphoreType.DMA((4,)),
            pltpu.SemaphoreType.DMA((4,)),
            *sems,
        ],
        compiler_params=pltpu.CompilerParams(
            collective_id=0, has_side_effects=True, vmem_limit_bytes=60 * 1024 * 1024
        ),
        name="panel",
    )(codes, cot, embed, first, second)


def expand_kernel(x_ref, sums_ref, embed_ref, block_ref, out_ref, first_out, second_out, first_ref, second_ref, done):
    moves = []

    def move(src, dst):
        copy = pltpu.make_async_copy(src, dst, done.at[len(moves)])
        copy.start()
        moves.append(copy)

    move(block_ref, out_ref)
    channels = embed_ref.shape[1]
    half = channels // 2
    flip = flip_matrix(channels)
    outer = x_ref[:channels]
    second_ref[0] = outer.astype(F32)
    move(second_ref.at[0], second_out.at[0])
    second_ref[2] = dot(dot(flip, outer).astype(BF16), flip)
    move(second_ref.at[2], second_out.at[2])
    inner = x_ref[channels : channels + half]
    second_ref[1, :half] = inner.astype(F32)
    second_ref[1, half:] = dot(dot(flip[half:, :half], inner).astype(BF16), flip)
    move(second_ref.at[1], second_out.at[1])
    sums = sums_ref[...]
    sums_flip = dot(sums, flip).astype(BF16)
    embed = embed_ref[...]
    for k in range(3):
        row = lax.broadcasted_iota(jnp.int32, (16, BASES), 0)
        col = lax.broadcasted_iota(jnp.int32, (16, BASES), 1)
        here = dot((row == BASES * k + col).astype(F32).astype(BF16), embed).astype(BF16)
        there = dot((row == BASES * (2 - k) + col).astype(F32).astype(BF16), embed).astype(BF16)
        there = dot(there, flip).astype(BF16)
        first_ref[k] = dot_rows(here, sums) + dot_rows(there, sums_flip)
        move(first_ref.at[k], first_out.at[k])
    for copy in moves:
        copy.wait()


def expand(x, sums, embed, block):
    channels = x.shape[1]
    shape = jax.ShapeDtypeStruct((3, channels, channels), F32)
    return pl.pallas_call(
        expand_kernel,
        out_shape=(jax.ShapeDtypeStruct(block.shape, BF16), shape, shape),
        in_specs=[VMEM, VMEM, VMEM, VMEM],
        out_specs=(ANY, ANY, ANY),
        scratch_shapes=[
            pltpu.VMEM(shape.shape, F32),
            pltpu.VMEM(shape.shape, F32),
            pltpu.SemaphoreType.DMA((7,)),
        ],
        compiler_params=pltpu.CompilerParams(vmem_limit_bytes=32 * 1024 * 1024),
        name="expand",
    )(x, sums, embed, block)


def local(codes, embed, first, second, cot):
    block, rows, sums = panel(codes, embed, first, second, cot)
    return expand(rows.reshape(-1, cot.shape[2]), sums, embed, block)


def solution(mesh):
    in_specs = (P("dp", "seq"), P(), P(), P(), P("dp", "seq", None))
    out_specs = (P("dp", "seq", None), P(), P())
    return jax.shard_map(local, mesh=mesh, in_specs=in_specs, out_specs=out_specs, check_vma=False)
```
